32 devices in a mesh: dp: 4 (over z), fsdp: 4 (over x, core), ctx: 2 (over y).
Axes of the slice: x: 2, y: 2, z: 4, core: 2. Of those that a mesh axis runs over, the one named last changes fastest.
Arguments:
- tokens: bfloat16 [16, 1024, 1024], P(('dp', 'fsdp'), 'ctx')
- bounds: int32 [16, 1024], P(('dp', 'fsdp'), 'ctx'), may hold values 0 or 1
- decay_rates: float32 [16], replicated, may hold values from 9.765625e-05 to 0.9
- w_query: bfloat16 [1024, 1024], P('fsdp')
- w_key: bfloat16 [1024, 1024], P('fsdp')
- w_up: bfloat16 [1024, 2048], P('fsdp'), may hold values from -0.1875 to 0.1875
- grad_out: bfloat16 [16, 1024, 2048], P(('dp', 'fsdp'), 'ctx'), may hold values from -6 to 6
Outputs:
- dechunked: bfloat16 [16, 1024, 2048], P(('dp', 'fsdp'), 'ctx')
- grad_tokens: bfloat16 [16, 1024, 1024], P(('dp', 'fsdp'), 'ctx')
- grad_query: float32 [1024, 1024], P('fsdp')
- grad_key: float32 [1024, 1024], P('fsdp')
- grad_up: float32 [1024, 2048], P('fsdp')
The draws below stay inside these ranges and needn't reach their ends.
All inputs are finite; a program needn't handle non-finite values. No bound on the sum of `bounds` on one device may be relied on, other than what follows from the above.
Results may differ from the reference program's by a relative error of at most 0.0049.
Values may be sent and summed in bfloat16 or wider, within the bound.
A program may use at most 128 MiB of HBM per device.

```python
import math
import jax
import jax.numpy as jnp
from jax import lax

D = 1024
E = 2048
HEADS = 16
SEQ = 1024
BATCH = 16


def draw_tokens(key, part):
    base = jax.random.fold_in(key, 11)
    first_key, second_key, third_key = jax.random.split(base, 3)
    noise = jax.random.normal(first_key, (BATCH, SEQ + 1, D), jnp.float32)
    own_part = jax.random.uniform(second_key, (BATCH, SEQ, 1), jnp.float32, 0.5, 1.0)
    shared_part = jax.random.uniform(third_key, (BATCH, SEQ, 1), jnp.float32, -1.0, 1.0)
    return (own_part * noise[:, 1:] + shared_part * noise[:, :-1]).astype(jnp.bfloat16)


def near_identity(key):
    noise = jax.random.normal(key, (D, D), jnp.float32)
    return (jnp.eye(D, dtype=jnp.float32) + noise * (0.5 / D ** 0.5)).astype(jnp.bfloat16)


def draw_w_query(key, part):
    return near_identity(jax.random.fold_in(key, 21))


def draw_w_key(key, part):
    return near_identity(jax.random.fold_in(key, 22))


def touch_ends(result, rng, smallest, top_value):
    extent = result.shape
    spot = [jax.random.randint(jax.random.fold_in(rng, axis), (), 0, extent[axis]) for axis in range(len(extent))]
    result = result.at[tuple(spot)].set(smallest)
    longest = extent.index(max(extent))
    spot[longest] = (spot[longest] + 1) % extent[longest]
    return result.at[tuple(spot)].set(top_value)


def steps_of(rng, extent, cuts, low, high):
    level = 1.0
    for position, parts in cuts:
        steps = jax.random.uniform(jax.random.fold_in(jax.random.fold_in(rng, 6), position), (parts,), jnp.float32, low / len(cuts), high / len(cuts))
        level = level * jnp.repeat(jnp.exp(steps), extent[position] // parts).reshape((-1,) + (1,) * (len(extent) - 1 - position))
    return level


def bell_draw(key, extent, spread, most, shards=(), kind=jnp.bfloat16):
    array = spread * jax.random.normal(key, extent, jnp.float32)
    if shards:
        array = array * steps_of(key, extent, shards, -0.22, 0.18)
    return jnp.clip(array, -most, most).astype(kind)


def setup_inputs(seed: int = 0) -> dict:
    key_list = jax.random.split(jax.random.key(seed), 8)
    return {
        "tokens": draw_tokens(jax.random.fold_in(key_list[7], 71), 0),
        "bounds": touch_ends((jax.random.randint(key_list[1], (BATCH, SEQ), 0, 6) < 1).astype(jnp.int32), jax.random.fold_in(key_list[1], 1), 0, 1),
        "decay_rates": jnp.clip(jnp.exp(jax.random.uniform(key_list[2], (HEADS,), jnp.float32, math.log(9.765625145519152e-05), math.log(0.9))), 9.765625145519152e-05, 0.9),
        "w_query": draw_w_query(jax.random.fold_in(key_list[7], 71), 0),
        "w_key": draw_w_key(jax.random.fold_in(key_list[7], 71), 0),
        "w_up": bell_draw(key_list[5], (D, E), D ** -0.5, 0.1875, ((0, 4),)),
        "grad_out": bell_draw(key_list[6], (BATCH, SEQ, E), 1.0, 6.0, ((0, 16), (1, 2))),
    }


epsilon = 1e-06

def one_sequence(tokens_row, bounds_row, grad_row, w_query, w_key, w_up, decay_rates):
    length = tokens_row.shape[0]
    model_width = w_query.shape[0]
    head_count = decay_rates.shape[0]
    queries = jnp.dot(tokens_row, w_query, preferred_element_type=jnp.float32)
    keys_now = jnp.dot(tokens_row, w_key, preferred_element_type=jnp.float32)
    values = jnp.dot(tokens_row, w_up, preferred_element_type=jnp.float32)
    keys_prev = jnp.concatenate([jnp.zeros((1, model_width), jnp.float32), keys_now[:-1]], 0)
    inv_query = lax.rsqrt(lax.optimization_barrier(jnp.sum(queries * queries, -1)) + epsilon)
    inv_key = lax.rsqrt(lax.optimization_barrier(jnp.sum(keys_prev * keys_prev, -1)) + epsilon)
    cosine = lax.optimization_barrier(jnp.sum(queries * keys_prev, -1)) * inv_query * inv_key
    opening = jnp.arange(length) == 0
    boundary_prob = jnp.where(opening, 1.0, 0.5 * (1.0 - cosine))
    marked = jnp.where(opening, 1.0, bounds_row.astype(jnp.float32))
    mix_rate = (marked * boundary_prob)[:, None] * decay_rates[None, :]
    value_groups = values.reshape(length, head_count, -1)

    def forward_step(carried, element):
        rate_now, value_now = element
        carried = rate_now[:, None] * value_now + (1.0 - rate_now[:, None]) * carried
        return (carried, carried)
    zero_state = jnp.zeros(value_groups.shape[1:], jnp.float32)
    _, states = lax.scan(forward_step, zero_state, (mix_rate, value_groups))
    states_prev = jnp.concatenate([zero_state[None], states[:-1]], 0)
    cotangent = grad_row.astype(jnp.float32).reshape(length, head_count, -1)

    def backward_step(carried, element):
        rate_now, incoming = element
        adjoint = incoming + carried
        return ((1.0 - rate_now[:, None]) * adjoint, adjoint)
    _, adjoints = lax.scan(backward_step, zero_state, (mix_rate, cotangent), reverse=True)
    d_values = (mix_rate[:, :, None] * adjoints).reshape(length, -1).astype(jnp.bfloat16)
    d_rate = lax.optimization_barrier(jnp.sum(adjoints * (value_groups - states_prev), -1))
    d_prob = jnp.where(opening, 0.0, marked * lax.optimization_barrier(jnp.sum(d_rate * decay_rates[None, :], -1)))
    d_cos = -0.5 * d_prob
    pair_scale = inv_query * inv_key
    d_query = (d_cos[:, None] * (keys_prev * pair_scale[:, None] - (cosine * inv_query * inv_query)[:, None] * queries)).astype(jnp.bfloat16)
    d_prev = d_cos[:, None] * (queries * pair_scale[:, None] - (cosine * inv_key * inv_key)[:, None] * keys_prev)
    d_key = jnp.concatenate([d_prev[1:], jnp.zeros((1, model_width), jnp.float32)], 0).astype(jnp.bfloat16)
    d_all = jnp.concatenate([d_query, d_key, d_values], 1)
    panels = jnp.concatenate([w_query, w_key, w_up], 1)
    d_tokens = lax.dot_general(d_all, panels, (((1,), (1,)), ((), ())), preferred_element_type=jnp.float32).astype(jnp.bfloat16)
    grads = lax.dot_general(tokens_row, d_all, (((0,), (0,)), ((), ())), preferred_element_type=jnp.float32)
    return (states.reshape(length, -1).astype(jnp.bfloat16), d_tokens, grads)

def reference(tokens, bounds, decay_rates, w_query, w_key, w_up, grad_out):
    model_width = w_query.shape[0]

    def sequence_step(grad_sum, element):
        tokens_row, bounds_row, grad_row = element
        dechunked_row, d_tokens, grads = one_sequence(tokens_row, bounds_row, grad_row, w_query, w_key, w_up, decay_rates)
        return (grad_sum + grads, (dechunked_row, d_tokens))
    initial = jnp.zeros((model_width, 2 * model_width + w_up.shape[1]), jnp.float32)
    grad_sum, (dechunked, grad_tokens) = lax.scan(sequence_step, initial, (tokens, bounds, grad_out))
    return (dechunked, grad_tokens, grad_sum[:, :model_width], grad_sum[:, model_width:2 * model_width], grad_sum[:, 2 * model_width:])
```

```python
import functools

import jax
import jax.numpy as jnp
from jax import lax
from jax.experimental import pallas as pl
from jax.experimental.pallas import tpu as pltpu
from jax.sharding import PartitionSpec as P

SPAN = 128
epsilon = 1e-06
F32 = jnp.float32
BF16 = jnp.bfloat16
LIMIT = 48 * 1024 * 1024


def call(kernel, grid, in_specs, out_specs, out_shape, scratch, flops, moved, name):
    return pl.pallas_call(
        kernel,
        grid=grid,
        in_specs=in_specs,
        out_specs=out_specs,
        out_shape=out_shape,
        scratch_shapes=scratch,
        name=name,
        compiler_params=pltpu.CompilerParams(vmem_limit_bytes=LIMIT),
        cost_estimate=pl.CostEstimate(flops=flops, bytes_accessed=moved, transcendentals=0),
    )


def whole(shape):
    return pl.BlockSpec(shape, lambda i: (0,) * len(shape))


def rows_of(tile, width):
    return pl.BlockSpec((tile, width), lambda i: (i, 0))


def mm(a, b):
    return lax.dot_general(a, b, (((1,), (0,)), ((), ())), preferred_element_type=F32)


def route_kernel(parts, width, *refs):
    tok, tok_prev, marked, opening = refs[:4]
    shards = refs[4 : 4 + parts]
    q_out, k_out, iq_out, ik_out, cos_out, mp_out = refs[4 + parts :]
    depth = shards[0].shape[0]
    q = k = None
    for p in range(parts):
        span = slice(p * depth, (p + 1) * depth)
        one_q = mm(tok[:, span], shards[p][:, :width])
        one_k = mm(tok_prev[:, span], shards[p][:, width:])
        q = one_q if q is None else q + one_q
        k = one_k if k is None else k + one_k
    iq = lax.rsqrt(jnp.sum(q * q, -1, keepdims=True) + epsilon)
    ik = lax.rsqrt(jnp.sum(k * k, -1, keepdims=True) + epsilon)
    cosine = jnp.sum(q * k, -1, keepdims=True) * iq * ik
    q_out[...] = q
    k_out[...] = k
    iq_out[...] = iq
    ik_out[...] = ik
    cos_out[...] = cosine
    prob = jnp.where(opening[...] > 0, 1.0, 0.5 * (1.0 - cosine))
    mp_out[...] = marked[...] * prob


def log_sums(rate):
    log_keep = jnp.log(1.0 - rate)
    row = lax.broadcasted_iota(jnp.int32, (SPAN, SPAN), 0)
    col = lax.broadcasted_iota(jnp.int32, (SPAN, SPAN), 1)
    lower = (row >= col).astype(F32)
    sums = jnp.dot(lower, log_keep, precision=lax.Precision.HIGHEST, preferred_element_type=F32)
    return log_keep, sums, row, col


def adjoint_kernel(heads, channels, mp, decay, cot, adj_out, tail_out, head_out, dec_out, carry, run):
    @pl.when(pl.program_id(0) == 0)
    def _():
        carry[...] = jnp.zeros_like(carry)
        run[...] = jnp.zeros_like(run)

    rate = mp[...] * decay[...]
    _, sums, row, col = log_sums(rate)
    sums_t = sums.T
    total = sums[SPAN - 1 : SPAN, :]
    tail = jnp.exp(total - sums)
    tail_out[...] = tail * jnp.exp(run[...])
    keep_first = 1.0 - rate[0:1, :]
    for h in range(heads):
        lanes = slice(h * channels, (h + 1) * channels)
        gap = sums_t[h : h + 1, :] - sums[:, h : h + 1]
        band = jnp.where(col >= row, jnp.exp(jnp.minimum(gap, 0.0)), 0.0)
        high = band.astype(BF16)
        low = (band - high.astype(F32)).astype(BF16)
        c = cot[:, lanes]
        adj = mm(high, c) + mm(low, c) + tail[:, h : h + 1] * carry[:, lanes]
        adj_out[:, lanes] = adj
        carry[:, lanes] = keep_first[:, h : h + 1] * adj[0:1, :]
    run[...] += total
    head_out[...] = carry[...]
    dec_out[...] = jnp.exp(run[...])


def value_grad_kernel(heads, channels, adj, tail, mp, decay, adj_in, dv_out):
    rate = mp[...] * decay[...]
    for h in range(heads):
        lanes = slice(h * channels, (h + 1) * channels)
        full = adj[:, lanes] + tail[:, h : h + 1] * adj_in[:, lanes]
        dv_out[:, lanes] = (rate[:, h : h + 1] * full).astype(BF16)


def state_kernel(heads, channels, mp, decay, values, st_out, diff_out, dec_out, decp_out, last_out, carry, run):
    @pl.when(pl.program_id(0) == 0)
    def _():
        carry[...] = jnp.zeros_like(carry)
        run[...] = jnp.zeros_like(run)

    rate = mp[...] * decay[...]
    log_keep, sums, row, col = log_sums(rate)
    sums_t = sums.T
    from_start = jnp.exp(sums)
    before = jnp.exp(run[...])
    dec_out[...] = from_start * before
    decp_out[...] = jnp.exp(sums - log_keep) * before
    top = lax.broadcasted_iota(jnp.int32, (SPAN, channels), 0) == 0
    for h in range(heads):
        lanes = slice(h * channels, (h + 1) * channels)
        gap = sums[:, h : h + 1] - sums_t[h : h + 1, :]
        band = jnp.where(row >= col, jnp.exp(jnp.minimum(gap, 0.0)), 0.0)
        high = band.astype(BF16)
        low = (band - high.astype(F32)).astype(BF16)
        v = values[:, lanes]
        x = rate[:, h : h + 1] * v
        x_high = x.astype(BF16)
        x_low = (x - x_high.astype(F32)).astype(BF16)
        came = carry[:, lanes]
        state = mm(high, x_high) + mm(low, x_high) + mm(high, x_low) + from_start[:, h : h + 1] * came
        st_out[:, lanes] = state
        diff_out[:, lanes] = v - jnp.where(top, came, pltpu.roll(state, 1, 0))
        carry[:, lanes] = state[SPAN - 1 : SPAN, :]
    run[...] += sums[SPAN - 1 : SPAN, :]
    last_out[...] = carry[...]


def finish_kernel(
    heads, channels, st, diff, adj, tail, dec, decp, decay, adj_in, st_in, q, k, iq, ik, cos, marked, opening,
    out, dq_out, dp_out,
):
    d_prob = None
    for h in range(heads):
        lanes = slice(h * channels, (h + 1) * channels)
        one = slice(h, h + 1)
        came = st_in[:, lanes]
        out[:, lanes] = (st[:, lanes] + dec[:, one] * came).astype(BF16)
        full = adj[:, lanes] + tail[:, one] * adj_in[:, lanes]
        part = decay[:, one] * jnp.sum(full * (diff[:, lanes] - decp[:, one] * came), -1, keepdims=True)
        d_prob = part if d_prob is None else d_prob + part
    d_prob = jnp.where(opening[...] > 0, 0.0, marked[...] * d_prob)
    d_cos = -0.5 * d_prob
    a, b, c = iq[...], ik[...], cos[...]
    scale = a * b
    dq_out[...] = (d_cos * (k[...] * scale - (c * a * a) * q[...])).astype(BF16)
    dp_out[...] = (d_cos * (q[...] * scale - (c * b * b) * k[...])).astype(BF16)


def token_grad_kernel(width, place, dq, dk, dv, *refs):
    del place
    qk, up, out = refs
    dims = (((1,), (1,)), ((), ()))
    total = lax.dot_general(dq[...], qk[:, :width], dims, preferred_element_type=F32)
    total += lax.dot_general(dk[...], qk[:, width:], dims, preferred_element_type=F32)
    total += lax.dot_general(dv[...], up[...], dims, preferred_element_type=F32)
    out[...] = total.astype(BF16)


def flipped(x, bit):
    n = lax.axis_size("fsdp")
    return lax.ppermute(x, "fsdp", [(i, i ^ bit) for i in range(n)])


def turned(x, axis, by):
    n = lax.axis_size(axis)
    return lax.ppermute(x, axis, [(i, (i + by) % n) for i in range(n)])


def shifted(x, axis, by):
    n = lax.axis_size(axis)
    return lax.ppermute(x, axis, [(i, i + by) for i in range(n) if 0 <= i + by < n])


def spread_sum(x, axis):
    n = lax.axis_size(axis)
    me = lax.axis_index(axis)
    k, rows, cols = x.shape
    cut = x.reshape(k, n, rows // n, cols)

    def block(i):
        return lax.dynamic_index_in_dim(cut, i, 1, False)

    total = block(me)
    for d in range(1, n):
        total = total + turned(block(lax.rem(me + d, n)).astype(BF16), axis, d).astype(F32)
    return total


def collect(x, axis):
    n = lax.axis_size(axis)
    me = lax.axis_index(axis)
    got = [x] + [turned(x, axis, n - e) for e in range(1, n)]
    twice = jnp.concatenate(got + got[:-1], 0)
    rows = x.shape[0]
    return lax.dynamic_slice_in_dim(twice, lax.rem(n - me, n) * rows, n * rows, 0)


def halve(x, bit):
    half = x.shape[0] // 2
    return x[:half] + flipped(x[half:].astype(BF16), bit).astype(F32)


def reduce_rows(left, right, bits, parts, ctx_first):
    depth = right.shape[0] * 2 // parts
    x = left + flipped(right, bits[0]).astype(F32)
    x = x.reshape(parts // 2, depth, x.shape[1])
    if ctx_first:
        x = spread_sum(x, "ctx")
    for bit in bits[1:]:
        x = halve(x, bit)
    if not ctx_first:
        x = spread_sum(x, "ctx")
    x = spread_sum(x, "dp")[0].astype(BF16)
    return collect(collect(x, "dp"), "ctx").astype(F32)


def per_device(tokens, bounds, decay_rates, w_query, w_key, w_up, grad_out):
    batch_local, length, width = tokens.shape
    hidden = w_up.shape[1]
    heads = decay_rates.shape[0]
    channels = hidden // heads
    blocks = length // SPAN
    parts = lax.axis_size("fsdp")
    count = lax.axis_size("ctx")
    me = lax.axis_index("fsdp")
    depth = width // parts
    levels = parts.bit_length() - 1
    bits = [1 << s for s in range(levels)]
    order = [sum(((p >> s) & 1) << (levels - 1 - s) for s in range(levels)) for p in range(parts)]

    held = {0: jnp.concatenate([w_query, w_key], 1)}
    held_up = {0: w_up}
    for store in (held, held_up):
        for j in sorted(range(1, parts), key=lambda j: (bin(j).count("1"), -j)):
            bit = j & -j
            store[j] = flipped(store[j ^ bit], bit)
    qk_shards = [held[j] for j in order]
    up_shards = [held_up[j] for j in order]

    tok = tokens.reshape(length, width)
    before = shifted(tok[-1:], "ctx", 1)
    tok_prev = jnp.concatenate([before, tok[:-1]], 0)

    def ordered(x):
        cols = [lax.dynamic_slice_in_dim(x, (me ^ j) * depth, depth, 1) for j in order]
        return jnp.concatenate(cols, 1)

    tok, tok_prev = ordered(tok), ordered(tok_prev)
    tok_t, prev_t = lax.optimization_barrier((tok.T, tok_prev.T))
    first = lax.axis_index("ctx") == 0
    opening_flag = jnp.logical_and(first, jnp.arange(length) == 0)
    marked = jnp.where(opening_flag, 1.0, bounds.reshape(length).astype(F32))[:, None]
    opening = opening_flag.astype(F32)[:, None]
    decay = decay_rates[None, :]
    cot = grad_out.reshape(length, hidden)

    shape = jax.ShapeDtypeStruct
    column = shape((length, 1), F32)
    tile = min(256, length)
    q, k, iq, ik, cosine, mp = call(
        functools.partial(route_kernel, parts, width),
        (length // tile,),
        [rows_of(tile, width)] * 2 + [rows_of(tile, 1)] * 2 + [whole((depth, 2 * width))] * parts,
        [rows_of(tile, width)] * 2 + [rows_of(tile, 1)] * 4,
        [shape((length, width), F32)] * 2 + [column] * 4,
        [],
        4 * length * width * width,
        4 * width * width + 12 * length * width,
        "route",
    )(tok, tok_prev, marked, opening, *qk_shards)

    def back(tile_width):
        return pl.BlockSpec((SPAN, tile_width), lambda i: (blocks - 1 - i, 0))

    by_head = shape((length, heads), F32)
    scratch = [pltpu.VMEM((1, hidden), F32), pltpu.VMEM((1, heads), F32)]
    adj, tail, head_row, device_decay = call(
        functools.partial(adjoint_kernel, heads, channels),
        (blocks,),
        [back(1), whole((1, heads)), back(hidden)],
        [back(hidden), back(heads), whole((1, hidden)), whole((1, heads))],
        [shape((length, hidden), F32), by_head, shape((1, hidden), F32), shape((1, heads), F32)],
        scratch,
        8 * length * SPAN * hidden,
        6 * length * hidden,
        "adjoint",
    )(mp, decay, cot)

    def carried(own, by):
        spread = jnp.repeat(device_decay, channels, axis=1)
        came = shifted(own, "ctx", by)
        for _ in range(count - 2):
            came = shifted(spread * came + own, "ctx", by)
        return came

    adj_in = carried(head_row, -1)
    d_values = call(
        functools.partial(value_grad_kernel, heads, channels),
        (blocks,),
        [rows_of(SPAN, hidden), rows_of(SPAN, heads), rows_of(SPAN, 1), whole((1, heads)), whole((1, hidden))],
        rows_of(SPAN, hidden),
        shape((length, hidden), BF16),
        [],
        4 * length * hidden,
        6 * length * hidden,
        "value_grad",
    )(adj, tail, mp, decay, adj_in)

    half_rows = width // 2

    def chain(x_t, d, ctx_first):
        right = mm(x_t[half_rows:], d).astype(BF16)
        left = mm(x_t[:half_rows], d)
        return reduce_rows(left, right, bits, parts, ctx_first)

    cut = hidden // 2
    up_a = chain(tok_t, d_values[:, :cut], False)
    up_b = chain(tok_t, d_values[:, cut:], True)

    up_full = jnp.concatenate(up_shards, 0)
    values = mm(tok, up_full)
    states, diff, dec, decp, last_row = call(
        functools.partial(state_kernel, heads, channels),
        (blocks,),
        [rows_of(SPAN, 1), whole((1, heads)), rows_of(SPAN, hidden)],
        [rows_of(SPAN, hidden)] * 2 + [rows_of(SPAN, heads)] * 2 + [whole((1, hidden))],
        [shape((length, hidden), F32)] * 2 + [by_head] * 2 + [shape((1, hidden), F32)],
        scratch,
        12 * length * SPAN * hidden,
        12 * length * hidden,
        "state",
    )(mp, decay, values)
    st_in = carried(last_row, 1)

    dechunked, d_query, d_prev = call(
        functools.partial(finish_kernel, heads, channels),
        (blocks,),
        [rows_of(SPAN, hidden)] * 3 + [rows_of(SPAN, heads)] * 3 + [whole((1, heads))]
        + [whole((1, hidden))] * 2 + [rows_of(SPAN, width)] * 2 + [rows_of(SPAN, 1)] * 5,
        [rows_of(SPAN, hidden)] + [rows_of(SPAN, width)] * 2,
        [shape((length, hidden), BF16)] + [shape((length, width), BF16)] * 2,
        [],
        20 * length * hidden,
        20 * length * hidden,
        "finish",
    )(states, diff, adj, tail, dec, decp, decay, adj_in, st_in, q, k, iq, ik, cosine, marked, opening)

    grad_query = chain(tok_t, d_query, False)
    grad_key = chain(prev_t, d_prev, True)

    after = shifted(d_prev[:1], "ctx", -1)
    d_key = jnp.concatenate([d_prev[1:], after], 0)
    qk_full = jnp.concatenate(qk_shards, 0)
    place = jnp.stack([me ^ j for j in order]).astype(jnp.int32)
    grad_tokens = pl.pallas_call(
        functools.partial(token_grad_kernel, width),
        grid_spec=pltpu.PrefetchScalarGridSpec(
            num_scalar_prefetch=1,
            grid=(parts,),
            in_specs=[
                pl.BlockSpec((length, width), lambda i, s: (0, 0)),
                pl.BlockSpec((length, width), lambda i, s: (0, 0)),
                pl.BlockSpec((length, hidden), lambda i, s: (0, 0)),
                pl.BlockSpec((depth, 2 * width), lambda i, s: (i, 0)),
                pl.BlockSpec((depth, hidden), lambda i, s: (i, 0)),
            ],
            out_specs=pl.BlockSpec((length, depth), lambda i, s: (0, s[i])),
        ),
        out_shape=shape((length, width), BF16),
        name="token_grad",
        compiler_params=pltpu.CompilerParams(vmem_limit_bytes=LIMIT),
        cost_estimate=pl.CostEstimate(
            flops=2 * length * width * (2 * width + hidden),
            bytes_accessed=2 * width * (2 * width + hidden),
            transcendentals=0,
        ),
    )(place, d_query, d_key, d_values, qk_full, up_full)
    return (
        dechunked.reshape(batch_local, length, hidden),
        grad_tokens.reshape(batch_local, length, width),
        grad_query,
        grad_key,
        jnp.concatenate([up_a, up_b], 1),
    )


def solution(mesh):
    return jax.shard_map(
        per_device,
        mesh=mesh,
        in_specs=(
            P(("dp", "fsdp"), "ctx", None),
            P(("dp", "fsdp"), "ctx"),
            P(),
            P("fsdp", None),
            P("fsdp", None),
            P("fsdp", None),
            P(("dp", "fsdp"), "ctx", None),
        ),
        out_specs=(
            P(("dp", "fsdp"), "ctx", None),
            P(("dp", "fsdp"), "ctx", None),
            P("fsdp", None),
            P("fsdp", None),
            P("fsdp", None),
        ),
        check_vma=False,
    )
```

```python
import functools

import jax
import jax.numpy as jnp
from jax import lax
from jax.experimental import pallas as pl
from jax.experimental.pallas import tpu as pltpu
from jax.sharding import PartitionSpec as P

SPAN = 128
epsilon = 1e-06
F32 = jnp.float32
BF16 = jnp.bfloat16
LIMIT = 48 * 1024 * 1024


def call(kernel, grid, in_specs, out_specs, out_shape, scratch, flops, moved, name):
    return pl.pallas_call(
        kernel,
        grid=grid,
        in_specs=in_specs,
        out_specs=out_specs,
        out_shape=out_shape,
        scratch_shapes=scratch,
        name=name,
        compiler_params=pltpu.CompilerParams(vmem_limit_bytes=LIMIT),
        cost_estimate=pl.CostEstimate(flops=flops, bytes_accessed=moved, transcendentals=0),
    )


def whole(shape):
    return pl.BlockSpec(shape, lambda i: (0,) * len(shape))


def rows_of(tile, width):
    return pl.BlockSpec((tile, width), lambda i: (i, 0))


def mm(a, b):
    return lax.dot_general(a, b, (((1,), (0,)), ((), ())), preferred_element_type=F32)


def route_kernel(parts, width, *refs):
    tok, tok_prev, marked, opening = refs[:4]
    shards = refs[4 : 4 + parts]
    q_out, k_out, iq_out, ik_out, cos_out, mp_out = refs[4 + parts :]
    depth = shards[0].shape[0]
    q = k = None
    for p in range(parts):
        span = slice(p * depth, (p + 1) * depth)
        one_q = mm(tok[:, span], shards[p][:, :width])
        one_k = mm(tok_prev[:, span], shards[p][:, width:])
        q = one_q if q is None else q + one_q
        k = one_k if k is None else k + one_k
    iq = lax.rsqrt(jnp.sum(q * q, -1, keepdims=True) + epsilon)
    ik = lax.rsqrt(jnp.sum(k * k, -1, keepdims=True) + epsilon)
    cosine = jnp.sum(q * k, -1, keepdims=True) * iq * ik
    q_out[...] = q
    k_out[...] = k
    iq_out[...] = iq
    ik_out[...] = ik
    cos_out[...] = cosine
    prob = jnp.where(opening[...] > 0, 1.0, 0.5 * (1.0 - cosine))
    mp_out[...] = marked[...] * prob


def log_sums(rate):
    log_keep = jnp.log(1.0 - rate)
    row = lax.broadcasted_iota(jnp.int32, (SPAN, SPAN), 0)
    col = lax.broadcasted_iota(jnp.int32, (SPAN, SPAN), 1)
    lower = (row >= col).astype(F32)
    sums = jnp.dot(lower, log_keep, precision=lax.Precision.HIGHEST, preferred_element_type=F32)
    return log_keep, sums, row, col


def value_kernel(parts, tok, *refs):
    depth = refs[0].shape[0]
    total = mm(tok[:, :depth], refs[0][...])
    for p in range(1, parts):
        total += mm(tok[:, p * depth : (p + 1) * depth], refs[p][...])
    refs[parts][...] = total


def adjoint_kernel(heads, channels, mp, decay, cot, adj_out, tail_out, head_out, dec_out, carry, run):
    @pl.when(pl.program_id(0) == 0)
    def _():
        carry[...] = jnp.zeros_like(carry)
        run[...] = jnp.zeros_like(run)

    rate = mp[...] * decay[...]
    _, sums, row, col = log_sums(rate)
    sums_t = sums.T
    total = sums[SPAN - 1 : SPAN, :]
    tail = jnp.exp(total - sums)
    tail_out[...] = tail * jnp.exp(run[...])
    keep_first = 1.0 - rate[0:1, :]
    for h in range(heads):
        lanes = slice(h * channels, (h + 1) * channels)
        gap = sums_t[h : h + 1, :] - sums[:, h : h + 1]
        band = jnp.where(col >= row, jnp.exp(jnp.minimum(gap, 0.0)), 0.0)
        high = band.astype(BF16)
        low = (band - high.astype(F32)).astype(BF16)
        c = cot[:, lanes]
        adj = mm(high, c) + mm(low, c) + tail[:, h : h + 1] * carry[:, lanes]
        adj_out[:, lanes] = adj
        carry[:, lanes] = keep_first[:, h : h + 1] * adj[0:1, :]
    run[...] += total
    head_out[...] = carry[...]
    dec_out[...] = jnp.exp(run[...])


def value_grad_kernel(heads, channels, adj, tail, mp, decay, adj_in, dv_out):
    rate = mp[...] * decay[...]
    for h in range(heads):
        lanes = slice(h * channels, (h + 1) * channels)
        full = adj[:, lanes] + tail[:, h : h + 1] * adj_in[:, lanes]
        dv_out[:, lanes] = (rate[:, h : h + 1] * full).astype(BF16)


def state_kernel(heads, channels, mp, decay, values, st_out, diff_out, dec_out, decp_out, last_out, carry, run):
    @pl.when(pl.program_id(0) == 0)
    def _():
        carry[...] = jnp.zeros_like(carry)
        run[...] = jnp.zeros_like(run)

    rate = mp[...] * decay[...]
    log_keep, sums, row, col = log_sums(rate)
    sums_t = sums.T
    from_start = jnp.exp(sums)
    before = jnp.exp(run[...])
    dec_out[...] = from_start * before
    decp_out[...] = jnp.exp(sums - log_keep) * before
    top = lax.broadcasted_iota(jnp.int32, (SPAN, channels), 0) == 0
    for h in range(heads):
        lanes = slice(h * channels, (h + 1) * channels)
        gap = sums[:, h : h + 1] - sums_t[h : h + 1, :]
        band = jnp.where(row >= col, jnp.exp(jnp.minimum(gap, 0.0)), 0.0)
        high = band.astype(BF16)
        low = (band - high.astype(F32)).astype(BF16)
        v = values[:, lanes]
        x = rate[:, h : h + 1] * v
        x_high = x.astype(BF16)
        x_low = (x - x_high.astype(F32)).astype(BF16)
        came = carry[:, lanes]
        state = mm(high, x_high) + mm(low, x_high) + mm(high, x_low) + from_start[:, h : h + 1] * came
        st_out[:, lanes] = state
        diff_out[:, lanes] = v - jnp.where(top, came, pltpu.roll(state, 1, 0))
        carry[:, lanes] = state[SPAN - 1 : SPAN, :]
    run[...] += sums[SPAN - 1 : SPAN, :]
    last_out[...] = carry[...]


def finish_kernel(
    heads, channels, st, diff, adj, tail, dec, decp, decay, adj_in, st_in, q, k, iq, ik, cos, marked, opening,
    out, dq_out, dp_out,
):
    total = None
    for h in range(heads):
        lanes = slice(h * channels, (h + 1) * channels)
        one = slice(h, h + 1)
        came = st_in[:, lanes]
        out[:, lanes] = (st[:, lanes] + dec[:, one] * came).astype(BF16)
        full = adj[:, lanes] + tail[:, one] * adj_in[:, lanes]
        part = decay[:, one] * (full * (diff[:, lanes] - decp[:, one] * came))
        total = part if total is None else total + part
    d_prob = jnp.sum(total, -1, keepdims=True)
    d_prob = jnp.where(opening[...] > 0, 0.0, marked[...] * d_prob)
    d_cos = -0.5 * d_prob
    a, b, c = iq[...], ik[...], cos[...]
    scale = a * b
    dq_out[...] = (d_cos * (k[...] * scale - (c * a * a) * q[...])).astype(BF16)
    dp_out[...] = (d_cos * (q[...] * scale - (c * b * b) * k[...])).astype(BF16)


def token_grad_kernel(width, parts, place, dq, dk, dv, *refs):
    out = refs[2 * parts]
    dims = (((1,), (1,)), ((), ()))
    for p in range(parts):
        @pl.when(pl.program_id(0) == p)
        def _(qk=refs[p], up=refs[parts + p]):
            total = lax.dot_general(dq[...], qk[:, :width], dims, preferred_element_type=F32)
            total += lax.dot_general(dk[...], qk[:, width:], dims, preferred_element_type=F32)
            total += lax.dot_general(dv[...], up[...], dims, preferred_element_type=F32)
            out[...] = total.astype(BF16)


def flipped(x, bit):
    n = lax.axis_size("fsdp")
    return lax.ppermute(x, "fsdp", [(i, i ^ bit) for i in range(n)])


def turned(x, axis, by):
    n = lax.axis_size(axis)
    return lax.ppermute(x, axis, [(i, (i + by) % n) for i in range(n)])


def shifted(x, axis, by):
    n = lax.axis_size(axis)
    return lax.ppermute(x, axis, [(i, i + by) for i in range(n) if 0 <= i + by < n])


def spread_sum(x, axis):
    n = lax.axis_size(axis)
    me = lax.axis_index(axis)
    k, rows, cols = x.shape
    cut = x.reshape(k, n, rows // n, cols)

    def block(i):
        return lax.dynamic_index_in_dim(cut, i, 1, False)

    total = block(me)
    for d in range(1, n):
        total = total + turned(block(lax.rem(me + d, n)).astype(BF16), axis, d).astype(F32)
    return total


def collect(x, axis):
    n = lax.axis_size(axis)
    me = lax.axis_index(axis)
    got = [x] + [turned(x, axis, n - e) for e in range(1, n)]
    twice = jnp.concatenate(got + got[:-1], 0)
    rows = x.shape[0]
    return lax.dynamic_slice_in_dim(twice, lax.rem(n - me, n) * rows, n * rows, 0)


def halve(x, bit):
    half = x.shape[0] // 2
    return x[:half] + flipped(x[half:].astype(BF16), bit).astype(F32)


def first_hop(left, right, bits, parts):
    x = left + flipped(right, bits[0]).astype(F32)
    return x.reshape(parts // 2, right.shape[0] * 2 // parts, x.shape[1])


def pair_hops(x, bits):
    for bit in bits[1:]:
        x = halve(x, bit)
    return x


def second_hop(x, bits, ctx_first):
    return spread_sum(x, "ctx") if ctx_first else pair_hops(x, bits)


def third_hop(x, bits, ctx_first):
    return pair_hops(x, bits) if ctx_first else spread_sum(x, "ctx")


def joint_sum(first, second):
    x = jnp.concatenate([first, second], 2)
    return spread_sum(x, "dp")[0].astype(BF16)


def per_device(tokens, bounds, decay_rates, w_query, w_key, w_up, grad_out):
    batch_local, length, width = tokens.shape
    hidden = w_up.shape[1]
    heads = decay_rates.shape[0]
    channels = hidden // heads
    blocks = length // SPAN
    parts = lax.axis_size("fsdp")
    count = lax.axis_size("ctx")
    me = lax.axis_index("fsdp")
    depth = width // parts
    levels = parts.bit_length() - 1
    bits = [1 << s for s in range(levels)]
    order = [sum(((p >> s) & 1) << (levels - 1 - s) for s in range(levels)) for p in range(parts)]

    held = {0: jnp.concatenate([w_query, w_key], 1)}
    others = sorted(range(1, parts), key=lambda j: (bin(j).count("1"), -j))
    for j in others:
        held[j] = flipped(held[j ^ (j & -j)], j & -j)
    w_up, *waited = lax.optimization_barrier((w_up, *[held[j] for j in others]))
    held.update(zip(others, waited))
    held_up = {0: w_up}
    for j in others:
        held_up[j] = flipped(held_up[j ^ (j & -j)], j & -j)
    qk_shards = [held[j] for j in order]
    up_shards = [held_up[j] for j in order]

    tok = tokens.reshape(length, width)
    before = shifted(tok[-1:], "ctx", 1)
    tok_prev = jnp.concatenate([before, tok[:-1]], 0)

    def ordered(x):
        cols = [lax.dynamic_slice_in_dim(x, (me ^ j) * depth, depth, 1) for j in order]
        return jnp.concatenate(cols, 1)

    tok, tok_prev = ordered(tok), ordered(tok_prev)
    tok_t, prev_t = lax.optimization_barrier((tok.T, tok_prev.T))
    first = lax.axis_index("ctx") == 0
    opening_flag = jnp.logical_and(first, jnp.arange(length) == 0)
    marked = jnp.where(opening_flag, 1.0, bounds.reshape(length).astype(F32))[:, None]
    opening = opening_flag.astype(F32)[:, None]
    decay = decay_rates[None, :]
    cot = grad_out.reshape(length, hidden)

    shape = jax.ShapeDtypeStruct
    column = shape((length, 1), F32)
    tile = min(256, length)
    q, k, iq, ik, cosine, mp = call(
        functools.partial(route_kernel, parts, width),
        (length // tile,),
        [rows_of(tile, width)] * 2 + [rows_of(tile, 1)] * 2 + [whole((depth, 2 * width))] * parts,
        [rows_of(tile, width)] * 2 + [rows_of(tile, 1)] * 4,
        [shape((length, width), F32)] * 2 + [column] * 4,
        [],
        4 * length * width * width,
        4 * width * width + 12 * length * width,
        "route",
    )(tok, tok_prev, marked, opening, *qk_shards)

    def back(tile_width):
        return pl.BlockSpec((SPAN, tile_width), lambda i: (blocks - 1 - i, 0))

    by_head = shape((length, heads), F32)
    scratch = [pltpu.VMEM((1, hidden), F32), pltpu.VMEM((1, heads), F32)]
    adj, tail, head_row, device_decay = call(
        functools.partial(adjoint_kernel, heads, channels),
        (blocks,),
        [back(1), whole((1, heads)), back(hidden)],
        [back(hidden), back(heads), whole((1, hidden)), whole((1, heads))],
        [shape((length, hidden), F32), by_head, shape((1, hidden), F32), shape((1, heads), F32)],
        scratch,
        8 * length * SPAN * hidden,
        6 * length * hidden,
        "adjoint",
    )(mp, decay, cot)

    def carried(own, by):
        spread = jnp.repeat(device_decay, channels, axis=1)
        came = shifted(own, "ctx", by)
        for _ in range(count - 2):
            came = shifted(spread * came + own, "ctx", by)
        return came

    adj_in = carried(head_row, -1)
    d_values = call(
        functools.partial(value_grad_kernel, heads, channels),
        (blocks,),
        [rows_of(SPAN, hidden), rows_of(SPAN, heads), rows_of(SPAN, 1), whole((1, heads)), whole((1, hidden))],
        rows_of(SPAN, hidden),
        shape((length, hidden), BF16),
        [],
        4 * length * hidden,
        6 * length * hidden,
        "value_grad",
    )(adj, tail, mp, decay, adj_in)

    half_rows = width // 2

    def terms(x_t, d):
        return mm(x_t[:half_rows], d), mm(x_t[half_rows:], d).astype(BF16)

    cut = hidden // 2
    terms_a = terms(tok_t, d_values[:, :cut])
    terms_b = terms(tok_t, d_values[:, cut:])
    up_a = first_hop(*terms_a, bits, parts)
    up_b = first_hop(*terms_b, bits, parts)
    up_a, up_b, up_shards = lax.optimization_barrier((up_a, up_b, up_shards))
    up_a = second_hop(up_a, bits, False)
    up_b = second_hop(up_b, bits, True)

    values = call(
        functools.partial(value_kernel, parts),
        (length // tile,),
        [rows_of(tile, width)] + [whole((depth, hidden))] * parts,
        rows_of(tile, hidden),
        shape((length, hidden), F32),
        [],
        2 * length * width * hidden,
        2 * width * hidden + 4 * length * hidden,
        "values",
    )(tok, *up_shards)
    states, diff, dec, decp, last_row = call(
        functools.partial(state_kernel, heads, channels),
        (blocks,),
        [rows_of(SPAN, 1), whole((1, heads)), rows_of(SPAN, hidden)],
        [rows_of(SPAN, hidden)] * 2 + [rows_of(SPAN, heads)] * 2 + [whole((1, hidden))],
        [shape((length, hidden), F32)] * 2 + [by_head] * 2 + [shape((1, hidden), F32)],
        scratch,
        12 * length * SPAN * hidden,
        12 * length * hidden,
        "state",
    )(mp, decay, values)
    st_in = carried(last_row, 1)

    dechunked, d_query, d_prev = call(
        functools.partial(finish_kernel, heads, channels),
        (blocks,),
        [rows_of(SPAN, hidden)] * 3 + [rows_of(SPAN, heads)] * 3 + [whole((1, heads))]
        + [whole((1, hidden))] * 2 + [rows_of(SPAN, width)] * 2 + [rows_of(SPAN, 1)] * 5,
        [rows_of(SPAN, hidden)] + [rows_of(SPAN, width)] * 2,
        [shape((length, hidden), BF16)] + [shape((length, width), BF16)] * 2,
        [],
        20 * length * hidden,
        20 * length * hidden,
        "finish",
    )(states, diff, adj, tail, dec, decp, decay, adj_in, st_in, q, k, iq, ik, cosine, marked, opening)

    up_a, up_b, d_query, d_prev = lax.optimization_barrier((up_a, up_b, d_query, d_prev))
    terms_q, terms_k = terms(tok_t, d_query), terms(prev_t, d_prev)
    terms_q, terms_k, d_query, d_prev = lax.optimization_barrier((terms_q, terms_k, d_query, d_prev))
    part_q = first_hop(*terms_q, bits, parts)
    part_k = first_hop(*terms_k, bits, parts)
    up_a = third_hop(up_a, bits, False)
    up_b = third_hop(up_b, bits, True)
    up_a, up_b, part_q, part_k = lax.optimization_barrier((up_a, up_b, part_q, part_k))
    up_joint = collect(joint_sum(up_a, up_b), "dp")
    part_q = third_hop(second_hop(part_q, bits, False), bits, False)
    part_k = third_hop(second_hop(part_k, bits, True), bits, True)
    qk_joint = joint_sum(part_q, part_k)
    up_joint, qk_joint = lax.optimization_barrier((up_joint, qk_joint))
    grad_up = collect(up_joint, "ctx").astype(F32)
    grad_qk = collect(collect(qk_joint, "dp"), "ctx").astype(F32)

    after = shifted(d_prev[:1], "ctx", -1)
    d_key = jnp.concatenate([d_prev[1:], after], 0)
    place = jnp.stack([me ^ j for j in order]).astype(jnp.int32)
    grad_tokens = pl.pallas_call(
        functools.partial(token_grad_kernel, width, parts),
        grid_spec=pltpu.PrefetchScalarGridSpec(
            num_scalar_prefetch=1,
            grid=(parts,),
            in_specs=[
                pl.BlockSpec((length, width), lambda i, s: (0, 0)),
                pl.BlockSpec((length, width), lambda i, s: (0, 0)),
                pl.BlockSpec((length, hidden), lambda i, s: (0, 0)),
            ]
            + [pl.BlockSpec((depth, 2 * width), lambda i, s: (0, 0))] * parts
            + [pl.BlockSpec((depth, hidden), lambda i, s: (0, 0))] * parts,
            out_specs=pl.BlockSpec((length, depth), lambda i, s: (0, s[i])),
        ),
        out_shape=shape((length, width), BF16),
        name="token_grad",
        compiler_params=pltpu.CompilerParams(vmem_limit_bytes=LIMIT),
        cost_estimate=pl.CostEstimate(
            flops=2 * length * width * (2 * width + hidden),
            bytes_accessed=2 * width * (2 * width + hidden),
            transcendentals=0,
        ),
    )(place, d_query, d_key, d_values, *qk_shards, *up_shards)
    return (
        dechunked.reshape(batch_local, length, hidden),
        grad_tokens.reshape(batch_local, length, width),
        grad_qk[:, :width],
        grad_qk[:, width:],
        grad_up,
    )


def solution(mesh):
    return jax.shard_map(
        per_device,
        mesh=mesh,
        in_specs=(
            P(("dp", "fsdp"), "ctx", None),
            P(("dp", "fsdp"), "ctx"),
            P(),
            P("fsdp", None),
            P("fsdp", None),
            P("fsdp", None),
            P(("dp", "fsdp"), "ctx", None),
        ),
        out_specs=(
            P(("dp", "fsdp"), "ctx", None),
            P(("dp", "fsdp"), "ctx", None),
            P("fsdp", None),
            P("fsdp", None),
            P("fsdp", None),
        ),
        check_vma=False,
    )
```

```python
import functools

import jax
import jax.numpy as jnp
from jax import lax
from jax.experimental import pallas as pl
from jax.experimental.pallas import tpu as pltpu
from jax.sharding import PartitionSpec as P

SPAN = 128
epsilon = 1e-06
F32 = jnp.float32
BF16 = jnp.bfloat16
LIMIT = 48 * 1024 * 1024


def call(kernel, grid, in_specs, out_specs, out_shape, scratch, flops, moved, name):
    return pl.pallas_call(
        kernel,
        grid=grid,
        in_specs=in_specs,
        out_specs=out_specs,
        out_shape=out_shape,
        scratch_shapes=scratch,
        name=name,
        compiler_params=pltpu.CompilerParams(vmem_limit_bytes=LIMIT),
        cost_estimate=pl.CostEstimate(flops=flops, bytes_accessed=moved, transcendentals=0),
    )


def whole(shape):
    return pl.BlockSpec(shape, lambda i: (0,) * len(shape))


def rows_of(tile, width):
    return pl.BlockSpec((tile, width), lambda i: (i, 0))


def mm(a, b):
    return lax.dot_general(a, b, (((1,), (0,)), ((), ())), preferred_element_type=F32)


def route_kernel(parts, width, *refs):
    tok, tok_prev, marked, opening = refs[:4]
    shards = refs[4 : 4 + parts]
    q_out, k_out, iq_out, ik_out, cos_out, mp_out = refs[4 + parts :]
    depth = shards[0].shape[0]
    q = k = None
    for p in range(parts):
        span = slice(p * depth, (p + 1) * depth)
        one_q = mm(tok[:, span], shards[p][:, :width])
        one_k = mm(tok_prev[:, span], shards[p][:, width:])
        q = one_q if q is None else q + one_q
        k = one_k if k is None else k + one_k
    iq = lax.rsqrt(jnp.sum(q * q, -1, keepdims=True) + epsilon)
    ik = lax.rsqrt(jnp.sum(k * k, -1, keepdims=True) + epsilon)
    cosine = jnp.sum(q * k, -1, keepdims=True) * iq * ik
    q_out[...] = q
    k_out[...] = k
    iq_out[...] = iq
    ik_out[...] = ik
    cos_out[...] = cosine
    prob = jnp.where(opening[...] > 0, 1.0, 0.5 * (1.0 - cosine))
    mp_out[...] = marked[...] * prob


def log_sums(rate):
    log_keep = jnp.log(1.0 - rate)
    row = lax.broadcasted_iota(jnp.int32, (SPAN, SPAN), 0)
    col = lax.broadcasted_iota(jnp.int32, (SPAN, SPAN), 1)
    lower = (row >= col).astype(F32)
    sums = jnp.dot(lower, log_keep, precision=lax.Precision.HIGHEST, preferred_element_type=F32)
    return log_keep, sums, row, col


def value_kernel(parts, tok, *refs):
    depth = refs[0].shape[0]
    total = mm(tok[:, :depth], refs[0][...])
    for p in range(1, parts):
        total += mm(tok[:, p * depth : (p + 1) * depth], refs[p][...])
    refs[parts][...] = total


def adjoint_kernel(heads, channels, mp, decay, cot, adj_out, tail_out, head_out, dec_out, carry, run):
    @pl.when(pl.program_id(0) == 0)
    def _():
        carry[...] = jnp.zeros_like(carry)
        run[...] = jnp.zeros_like(run)

    rate = mp[...] * decay[...]
    _, sums, row, col = log_sums(rate)
    sums_t = sums.T
    total = sums[SPAN - 1 : SPAN, :]
    tail = jnp.exp(total - sums)
    tail_out[...] = tail * jnp.exp(run[...])
    keep_first = 1.0 - rate[0:1, :]
    for h in range(heads):
        lanes = slice(h * channels, (h + 1) * channels)
        gap = sums_t[h : h + 1, :] - sums[:, h : h + 1]
        band = jnp.where(col >= row, jnp.exp(jnp.minimum(gap, 0.0)), 0.0)
        high = band.astype(BF16)
        low = (band - high.astype(F32)).astype(BF16)
        c = cot[:, lanes]
        adj = mm(high, c) + mm(low, c) + tail[:, h : h + 1] * carry[:, lanes]
        adj_out[:, lanes] = adj
        carry[:, lanes] = keep_first[:, h : h + 1] * adj[0:1, :]
    run[...] += total
    head_out[...] = carry[...]
    dec_out[...] = jnp.exp(run[...])


def value_grad_kernel(heads, channels, adj, tail, mp, decay, adj_in, dv_out):
    rate = mp[...] * decay[...]
    for h in range(heads):
        lanes = slice(h * channels, (h + 1) * channels)
        full = adj[:, lanes] + tail[:, h : h + 1] * adj_in[:, lanes]
        dv_out[:, lanes] = (rate[:, h : h + 1] * full).astype(BF16)


def state_kernel(heads, channels, mp, decay, values, st_out, diff_out, dec_out, decp_out, last_out, carry, run):
    @pl.when(pl.program_id(0) == 0)
    def _():
        carry[...] = jnp.zeros_like(carry)
        run[...] = jnp.zeros_like(run)

    rate = mp[...] * decay[...]
    log_keep, sums, row, col = log_sums(rate)
    sums_t = sums.T
    from_start = jnp.exp(sums)
    before = jnp.exp(run[...])
    dec_out[...] = from_start * before
    decp_out[...] = jnp.exp(sums - log_keep) * before
    top = lax.broadcasted_iota(jnp.int32, (SPAN, channels), 0) == 0
    for h in range(heads):
        lanes = slice(h * channels, (h + 1) * channels)
        gap = sums[:, h : h + 1] - sums_t[h : h + 1, :]
        band = jnp.where(row >= col, jnp.exp(jnp.minimum(gap, 0.0)), 0.0)
        high = band.astype(BF16)
        low = (band - high.astype(F32)).astype(BF16)
        v = values[:, lanes]
        x = rate[:, h : h + 1] * v
        x_high = x.astype(BF16)
        x_low = (x - x_high.astype(F32)).astype(BF16)
        came = carry[:, lanes]
        state = mm(high, x_high) + mm(low, x_high) + mm(high, x_low) + from_start[:, h : h + 1] * came
        st_out[:, lanes] = state
        diff_out[:, lanes] = v - jnp.where(top, came, pltpu.roll(state, 1, 0))
        carry[:, lanes] = state[SPAN - 1 : SPAN, :]
    run[...] += sums[SPAN - 1 : SPAN, :]
    last_out[...] = carry[...]


def finish_kernel(
    heads, channels, st, diff, adj, tail, dec, decp, decay, adj_in, st_in, q, k, iq, ik, cos, marked, opening,
    out, dq_out, dp_out,
):
    total = None
    for h in range(heads):
        lanes = slice(h * channels, (h + 1) * channels)
        one = slice(h, h + 1)
        came = st_in[:, lanes]
        out[:, lanes] = (st[:, lanes] + dec[:, one] * came).astype(BF16)
        full = adj[:, lanes] + tail[:, one] * adj_in[:, lanes]
        part = decay[:, one] * (full * (diff[:, lanes] - decp[:, one] * came))
        total = part if total is None else total + part
    d_prob = jnp.sum(total, -1, keepdims=True)
    d_prob = jnp.where(opening[...] > 0, 0.0, marked[...] * d_prob)
    d_cos = -0.5 * d_prob
    a, b, c = iq[...], ik[...], cos[...]
    scale = a * b
    dq_out[...] = (d_cos * (k[...] * scale - (c * a * a) * q[...])).astype(BF16)
    dp_out[...] = (d_cos * (q[...] * scale - (c * b * b) * k[...])).astype(BF16)


def token_grad_kernel(width, parts, place, dq, dk, dv, *refs):
    out = refs[2 * parts]
    dims = (((1,), (1,)), ((), ()))
    for p in range(parts):
        @pl.when(pl.program_id(0) == p)
        def _(qk=refs[p], up=refs[parts + p]):
            total = lax.dot_general(dq[...], qk[:, :width], dims, preferred_element_type=F32)
            total += lax.dot_general(dk[...], qk[:, width:], dims, preferred_element_type=F32)
            total += lax.dot_general(dv[...], up[...], dims, preferred_element_type=F32)
            out[...] = total.astype(BF16)


def flipped(x, bit):
    n = lax.axis_size("fsdp")
    return lax.ppermute(x, "fsdp", [(i, i ^ bit) for i in range(n)])


def turned(x, axis, by):
    n = lax.axis_size(axis)
    return lax.ppermute(x, axis, [(i, (i + by) % n) for i in range(n)])


def shifted(x, axis, by):
    n = lax.axis_size(axis)
    return lax.ppermute(x, axis, [(i, i + by) for i in range(n) if 0 <= i + by < n])


def spread_sum(x, axis):
    n = lax.axis_size(axis)
    me = lax.axis_index(axis)
    k, rows, cols = x.shape
    cut = x.reshape(k, n, rows // n, cols)

    def block(i):
        return lax.dynamic_index_in_dim(cut, i, 1, False)

    total = block(me)
    for d in range(1, n):
        total = total + turned(block(lax.rem(me + d, n)).astype(BF16), axis, d).astype(F32)
    return total


def collect(x, axis):
    n = lax.axis_size(axis)
    me = lax.axis_index(axis)
    got = [x] + [turned(x, axis, n - e) for e in range(1, n)]
    twice = jnp.concatenate(got + got[:-1], 0)
    rows = x.shape[0]
    return lax.dynamic_slice_in_dim(twice, lax.rem(n - me, n) * rows, n * rows, 0)


def halve(x, bit):
    half = x.shape[0] // 2
    return x[:half] + flipped(x[half:].astype(BF16), bit).astype(F32)


def first_hop(left, right, bits, parts):
    x = left + flipped(right, bits[0]).astype(F32)
    return x.reshape(parts // 2, right.shape[0] * 2 // parts, x.shape[1])


def pair_hops(x, bits):
    for bit in bits[1:]:
        x = halve(x, bit)
    return x


def second_hop(x, bits, ctx_first):
    return spread_sum(x, "ctx") if ctx_first else pair_hops(x, bits)


def third_hop(x, bits, ctx_first):
    return pair_hops(x, bits) if ctx_first else spread_sum(x, "ctx")


def joint_sum(first, second):
    x = jnp.concatenate([first, second], 2)
    return spread_sum(x, "dp")[0].astype(BF16)


def per_device(tokens, bounds, decay_rates, w_query, w_key, w_up, grad_out):
    batch_local, length, width = tokens.shape
    hidden = w_up.shape[1]
    heads = decay_rates.shape[0]
    channels = hidden // heads
    blocks = length // SPAN
    parts = lax.axis_size("fsdp")
    count = lax.axis_size("ctx")
    me = lax.axis_index("fsdp")
    depth = width // parts
    levels = parts.bit_length() - 1
    bits = [1 << s for s in range(levels)]
    order = [sum(((p >> s) & 1) << (levels - 1 - s) for s in range(levels)) for p in range(parts)]

    held = {0: jnp.concatenate([w_query, w_key], 1)}
    others = sorted(range(1, parts), key=lambda j: (bin(j).count("1"), -j))
    for j in others:
        held[j] = flipped(held[j ^ (j & -j)], j & -j)
    w_up, *waited = lax.optimization_barrier((w_up, *[held[j] for j in others]))
    held.update(zip(others, waited))
    held_up = {0: w_up}
    for j in others:
        held_up[j] = flipped(held_up[j ^ (j & -j)], j & -j)
    qk_shards = [held[j] for j in order]
    up_shards = [held_up[j] for j in order]

    tok = tokens.reshape(length, width)
    before = shifted(tok[-1:], "ctx", 1)
    tok_prev = jnp.concatenate([before, tok[:-1]], 0)

    def ordered(x):
        cols = [lax.dynamic_slice_in_dim(x, (me ^ j) * depth, depth, 1) for j in order]
        return jnp.concatenate(cols, 1)

    tok, tok_prev = ordered(tok), ordered(tok_prev)
    tok_t, prev_t = lax.optimization_barrier((tok.T, tok_prev.T))
    first = lax.axis_index("ctx") == 0
    opening_flag = jnp.logical_and(first, jnp.arange(length) == 0)
    marked = jnp.where(opening_flag, 1.0, bounds.reshape(length).astype(F32))[:, None]
    opening = opening_flag.astype(F32)[:, None]
    decay = decay_rates[None, :]
    cot = grad_out.reshape(length, hidden)

    shape = jax.ShapeDtypeStruct
    column = shape((length, 1), F32)
    tile = min(256, length)
    q, k, iq, ik, cosine, mp = call(
        functools.partial(route_kernel, parts, width),
        (length // tile,),
        [rows_of(tile, width)] * 2 + [rows_of(tile, 1)] * 2 + [whole((depth, 2 * width))] * parts,
        [rows_of(tile, width)] * 2 + [rows_of(tile, 1)] * 4,
        [shape((length, width), F32)] * 2 + [column] * 4,
        [],
        4 * length * width * width,
        4 * width * width + 12 * length * width,
        "route",
    )(tok, tok_prev, marked, opening, *qk_shards)

    def back(tile_width):
        return pl.BlockSpec((SPAN, tile_width), lambda i: (blocks - 1 - i, 0))

    by_head = shape((length, heads), F32)
    scratch = [pltpu.VMEM((1, hidden), F32), pltpu.VMEM((1, heads), F32)]
    adj, tail, head_row, device_decay = call(
        functools.partial(adjoint_kernel, heads, channels),
        (blocks,),
        [back(1), whole((1, heads)), back(hidden)],
        [back(hidden), back(heads), whole((1, hidden)), whole((1, heads))],
        [shape((length, hidden), F32), by_head, shape((1, hidden), F32), shape((1, heads), F32)],
        scratch,
        8 * length * SPAN * hidden,
        6 * length * hidden,
        "adjoint",
    )(mp, decay, cot)

    def carried(own, by):
        spread = jnp.repeat(device_decay, channels, axis=1)
        came = shifted(own, "ctx", by)
        for _ in range(count - 2):
            came = shifted(spread * came + own, "ctx", by)
        return came

    adj_in = carried(head_row, -1)
    d_values = call(
        functools.partial(value_grad_kernel, heads, channels),
        (blocks,),
        [rows_of(SPAN, hidden), rows_of(SPAN, heads), rows_of(SPAN, 1), whole((1, heads)), whole((1, hidden))],
        rows_of(SPAN, hidden),
        shape((length, hidden), BF16),
        [],
        4 * length * hidden,
        6 * length * hidden,
        "value_grad",
    )(adj, tail, mp, decay, adj_in)

    half_rows = width // 2

    def terms(x_t, d):
        return mm(x_t[:half_rows], d), mm(x_t[half_rows:], d).astype(BF16)

    cut = hidden // 2
    terms_a = terms(tok_t, d_values[:, :cut])
    terms_b = terms(tok_t, d_values[:, cut:])
    up_a = first_hop(*terms_a, bits, parts)
    up_b = first_hop(*terms_b, bits, parts)
    up_a, up_b, up_shards = lax.optimization_barrier((up_a, up_b, up_shards))
    up_a = second_hop(up_a, bits, False)
    up_b = second_hop(up_b, bits, True)

    values = call(
        functools.partial(value_kernel, parts),
        (length // tile,),
        [rows_of(tile, width)] + [whole((depth, hidden))] * parts,
        rows_of(tile, hidden),
        shape((length, hidden), F32),
        [],
        2 * length * width * hidden,
        2 * width * hidden + 4 * length * hidden,
        "values",
    )(tok, *up_shards)
    states, diff, dec, decp, last_row = call(
        functools.partial(state_kernel, heads, channels),
        (blocks,),
        [rows_of(SPAN, 1), whole((1, heads)), rows_of(SPAN, hidden)],
        [rows_of(SPAN, hidden)] * 2 + [rows_of(SPAN, heads)] * 2 + [whole((1, hidden))],
        [shape((length, hidden), F32)] * 2 + [by_head] * 2 + [shape((1, hidden), F32)],
        scratch,
        12 * length * SPAN * hidden,
        12 * length * hidden,
        "state",
    )(mp, decay, values)
    st_in = carried(last_row, 1)

    dechunked, d_query, d_prev = call(
        functools.partial(finish_kernel, heads, channels),
        (blocks,),
        [rows_of(SPAN, hidden)] * 3 + [rows_of(SPAN, heads)] * 3 + [whole((1, heads))]
        + [whole((1, hidden))] * 2 + [rows_of(SPAN, width)] * 2 + [rows_of(SPAN, 1)] * 5,
        [rows_of(SPAN, hidden)] + [rows_of(SPAN, width)] * 2,
        [shape((length, hidden), BF16)] + [shape((length, width), BF16)] * 2,
        [],
        20 * length * hidden,
        20 * length * hidden,
        "finish",
    )(states, diff, adj, tail, dec, decp, decay, adj_in, st_in, q, k, iq, ik, cosine, marked, opening)

    up_a, up_b, d_query, d_prev = lax.optimization_barrier((up_a, up_b, d_query, d_prev))
    terms_q, terms_k = terms(tok_t, d_query), terms(prev_t, d_prev)
    terms_q, terms_k, d_query, d_prev = lax.optimization_barrier((terms_q, terms_k, d_query, d_prev))
    part_q = first_hop(*terms_q, bits, parts)
    part_k = first_hop(*terms_k, bits, parts)
    up_a = third_hop(up_a, bits, False)
    up_b = third_hop(up_b, bits, True)
    part_q = second_hop(part_q, bits, False)
    part_k = second_hop(part_k, bits, True)
    up_a, up_b, part_q, part_k = lax.optimization_barrier((up_a, up_b, part_q, part_k))
    up_joint = collect(joint_sum(up_a, up_b), "dp")
    part_q = third_hop(part_q, bits, False)
    part_k = third_hop(part_k, bits, True)
    qk_joint = joint_sum(part_q, part_k)
    up_joint, qk_joint = lax.optimization_barrier((up_joint, qk_joint))
    grad_up = collect(up_joint, "ctx").astype(F32)
    grad_qk = collect(collect(qk_joint, "dp"), "ctx").astype(F32)

    after = shifted(d_prev[:1], "ctx", -1)
    d_key = jnp.concatenate([d_prev[1:], after], 0)
    place = jnp.stack([me ^ j for j in order]).astype(jnp.int32)
    grad_tokens = pl.pallas_call(
        functools.partial(token_grad_kernel, width, parts),
        grid_spec=pltpu.PrefetchScalarGridSpec(
            num_scalar_prefetch=1,
            grid=(parts,),
            in_specs=[
                pl.BlockSpec((length, width), lambda i, s: (0, 0)),
                pl.BlockSpec((length, width), lambda i, s: (0, 0)),
                pl.BlockSpec((length, hidden), lambda i, s: (0, 0)),
            ]
            + [pl.BlockSpec((depth, 2 * width), lambda i, s: (0, 0))] * parts
            + [pl.BlockSpec((depth, hidden), lambda i, s: (0, 0))] * parts,
            out_specs=pl.BlockSpec((length, depth), lambda i, s: (0, s[i])),
        ),
        out_shape=shape((length, width), BF16),
        name="token_grad",
        compiler_params=pltpu.CompilerParams(vmem_limit_bytes=LIMIT),
        cost_estimate=pl.CostEstimate(
            flops=2 * length * width * (2 * width + hidden),
            bytes_accessed=2 * width * (2 * width + hidden),
            transcendentals=0,
        ),
    )(place, d_query, d_key, d_values, *qk_shards, *up_shards)
    return (
        dechunked.reshape(batch_local, length, hidden),
        grad_tokens.reshape(batch_local, length, width),
        grad_qk[:, :width],
        grad_qk[:, width:],
        grad_up,
    )


def solution(mesh):
    return jax.shard_map(
        per_device,
        mesh=mesh,
        in_specs=(
            P(("dp", "fsdp"), "ctx", None),
            P(("dp", "fsdp"), "ctx"),
            P(),
            P("fsdp", None),
            P("fsdp", None),
            P("fsdp", None),
            P(("dp", "fsdp"), "ctx", None),
        ),
        out_specs=(
            P(("dp", "fsdp"), "ctx", None),
            P(("dp", "fsdp"), "ctx", None),
            P("fsdp", None),
            P("fsdp", None),
            P("fsdp", None),
        ),
        check_vma=False,
    )
```
